32 devices in a mesh: feat: 8 (over z, x), pair: 4 (over y, core).
Axes of the slice: x: 2, y: 2, z: 4, core: 2. Of those that a mesh axis runs over, the one named last changes fastest.
Arguments:
- resid: bfloat16 [4, 1024, 2048], P('pair'), may hold values from -6 to 6
- enc_weight: bfloat16 [4, 2048, 16384], P('pair', None, 'feat'), may hold values from -0.125 to 0.125
- enc_bias: float32 [4, 16384], P('pair', 'feat'), may hold values from -3 to 3
- active: int32 [4, 1024, 64], P('pair'), may hold values from 0 to 16383, all different within a row
- dec_weight: bfloat16 [4, 4, 16384, 2048], P('pair', None, 'feat'), may hold values from -0.75 to 0.75
- dec_bias: float32 [4, 2048], P('pair'), may hold values from -3 to 3
- target: bfloat16 [4, 1024, 2048], P('pair', 'feat'), may hold values from -6 to 6
Outputs:
- error: float32 [4, 1024, 2048], P('pair', 'feat')
- dec_grad: bfloat16 [4, 4, 16384, 2048], P('pair', None, 'feat')
The draws below stay inside these ranges and needn't reach their ends.
Inputs may be any that keep to these rules, and one draw needn't show every extreme that they name: `active`: within one layer, the 64 indices of a token are distinct; every feature number occurs somewhere in the array.
All inputs are finite; a program needn't handle non-finite values.
Results may differ from the reference program's by a relative error of at most 0.0058.
Values may be sent and summed in bfloat16 or wider, within the bound.
No kernel may reach another device: no remote copies, remote signals or barrier semaphores. Data moves between devices by JAX's collectives and lax.ppermute only.
A program may use at most 192 MiB of HBM per device.

```python
import jax
import jax.numpy as jnp
from jax import lax

D = 2048
F = 16384
LAYERS = 4
K = 64
TOK = 1024


def block_scale(key, extent, cuts, least, top_value):
    def one(position, blocks):
        heights = jax.random.uniform(jax.random.fold_in(jax.random.fold_in(key, 6), position), (blocks,), jnp.float32, least / len(cuts), top_value / len(cuts))
        return jnp.repeat(jnp.exp(heights), extent[position] // blocks).reshape((-1,) + (1,) * (len(extent) - position - 1))

    factor_of = one(*cuts[0])
    for cut in cuts[1:]:
        factor_of = factor_of * one(*cut)
    return factor_of


def picks_of(key, rows, amount, top, lift):
    order = jax.random.permutation(jax.random.fold_in(key, 1), amount)
    favour = order
    for power in range(3):
        favour = favour * favour // amount
    favour = favour * lift // amount
    lots = jax.random.randint(jax.random.fold_in(key, 2), (rows, amount), 0, 4096) + favour
    holders = jax.random.permutation(jax.random.fold_in(key, 3), rows)[jnp.arange(amount) % rows]
    lots = jnp.where(jnp.arange(rows)[:, None] == holders[None, :], 1 << 14, lots)
    priority = lots * amount + jnp.arange(amount)
    return lax.top_k(priority.astype(jnp.int32), top)[1].astype(jnp.int32)


def scatter_about(stream_key, dims, spread, limit, split=(), dtype=jnp.bfloat16):
    drawn = jax.random.normal(stream_key, dims, jnp.float32) * spread
    if len(split) > 0:
        drawn = block_scale(stream_key, dims, split, -0.22, 0.18) * drawn
    return jnp.clip(drawn, min=-limit, max=limit).astype(dtype)


def setup_inputs(seed: int = 0) -> dict:
    keys = jax.random.split(jax.random.key(seed), 8)
    return {
        "resid": scatter_about(keys[0], (LAYERS, TOK, D), 1.0, 6.0, ((0, 4),)),
        "enc_weight": scatter_about(keys[1], (LAYERS, D, F), D ** -0.5, 0.125, ((0, 4), (2, 8))),
        "enc_bias": scatter_about(keys[2], (LAYERS, F), 0.5, 3.0, ((0, 4), (1, 8)), jnp.float32),
        "active": picks_of(keys[3], LAYERS * TOK, F, K, 32).reshape((LAYERS, TOK, K)),
        "dec_weight": scatter_about(keys[4], (LAYERS, LAYERS, F, D), K ** -0.5, 0.75, ((0, 4), (2, 8))),
        "dec_bias": scatter_about(keys[5], (LAYERS, D), 0.5, 3.0, ((0, 4),), jnp.float32),
        "target": scatter_about(keys[6], (LAYERS, TOK, D), 1.0, 6.0, ((0, 4), (1, 8))),
    }


def source_values(resid_layer, enc_layer, bias_layer, index_layer):
    columns = jnp.take(jnp.transpose(enc_layer), index_layer, axis=0)
    pre_act = jnp.einsum("td,tkd->tk", resid_layer.astype(jnp.float32), columns.astype(jnp.float32))
    pre_act = pre_act + jnp.take(bias_layer, index_layer)
    return jnp.maximum(pre_act, 0.0).astype(jnp.bfloat16)


def reference(resid, enc_weight, enc_bias, active, dec_weight, dec_bias, target):
    values = []
    for source in range(LAYERS):
        computed = source_values(resid[source], enc_weight[source], enc_bias[source], active[source])
        values.append(lax.optimization_barrier(computed).astype(jnp.float32))
    errors = []
    grad_table = []
    for dest in range(LAYERS):
        partial_value = jnp.zeros((TOK, D), jnp.float32)
        for source in range(dest + 1):
            picked = jnp.take(dec_weight[dest, source], active[source], axis=0)
            partial_value = partial_value + jnp.einsum("tk,tkd->td", values[source], picked.astype(jnp.float32))
        error_now = partial_value + dec_bias[dest][None, :] - target[dest].astype(jnp.float32)
        errors.append(error_now)
        rounded = lax.optimization_barrier(error_now.astype(jnp.bfloat16)).astype(jnp.float32)
        grad_row = []
        for source in range(LAYERS):
            if source <= dest:
                terms = values[source][:, :, None] * rounded[:, None, :]
                summed = jnp.zeros((F, D), jnp.float32).at[active[source]].add(terms)
                grad_row.append(summed.astype(jnp.bfloat16))
            else:
                grad_row.append(jnp.zeros((F, D), jnp.bfloat16))
        grad_table.append(jnp.stack(grad_row))
    return jnp.stack(errors), jnp.stack(grad_table)
```

```python
import functools

import jax
import jax.numpy as jnp
from jax import lax
from jax.experimental import pallas as pl
from jax.experimental.pallas import tpu as pltpu
from jax.sharding import PartitionSpec as P

LANES = 128
ROWS = 8
SLOTS = 32
FAR = 32767
VMEM_BYTES = 40 * 1024 * 1024
SMALL_BYTES = 8 * 1024 * 1024
PIECE = 512
CHUNK = 1024


def params(limit=VMEM_BYTES):
    return pltpu.CompilerParams(vmem_limit_bytes=limit)


def encode_kernel(resid_ref, weight_ref, bias_ref, slot_ref, out_ref, pre_ref, picked_ref, index_ref):
    step = pl.program_id(0)
    tokens = resid_ref.shape[0]
    width = weight_ref.shape[1]
    slots = slot_ref.shape[1]
    groups = width // LANES

    @pl.when(step == 0)
    def _():
        picked_ref[...] = jnp.zeros_like(picked_ref)
        pre_ref[1] = jnp.zeros_like(pre_ref[1])
        index_ref[...] = jnp.full_like(index_ref, FAR)
        index_ref[:, :slots] = slot_ref[...]

    now = lax.rem(step, 2)
    before = 1 - now
    pre_ref[now] = (
        jnp.dot(resid_ref[...], weight_ref[...], preferred_element_type=jnp.float32)
        + bias_ref[...]
    )
    first = (step - 1) * groups
    for row in range(0, tokens, ROWS):
        rows = pl.ds(row, ROWS)
        index = index_ref[rows, :]
        group = (index >> 7) - first
        lane = index & (LANES - 1)
        picked = picked_ref[rows, :]
        for part in range(groups):
            source = pre_ref[before, rows, part * LANES : (part + 1) * LANES]
            found = jnp.take_along_axis(source, lane, axis=1)
            picked = jnp.where(group == part, found, picked)
        picked_ref[rows, :] = picked

    @pl.when(step == pl.num_programs(0) - 1)
    def _():
        out_ref[...] = jnp.maximum(picked_ref[:, :slots], 0.0).astype(out_ref.dtype)


def encode(resid, weight, bias, slot_index):
    tokens, depth = resid.shape
    features = weight.shape[1]
    slots = slot_index.shape[1]
    width = min(256, features)
    steps = features // width
    return pl.pallas_call(
        encode_kernel,
        grid=(steps + 1,),
        in_specs=[
            pl.BlockSpec((tokens, depth), lambda i: (0, 0)),
            pl.BlockSpec((depth, width), lambda i: (0, jnp.minimum(i, steps - 1))),
            pl.BlockSpec((1, width), lambda i: (0, jnp.minimum(i, steps - 1))),
            pl.BlockSpec((tokens, slots), lambda i: (0, 0)),
        ],
        out_specs=pl.BlockSpec((tokens, slots), lambda i: (0, 0)),
        out_shape=jax.ShapeDtypeStruct((tokens, slots), jnp.bfloat16),
        scratch_shapes=[
            pltpu.VMEM((2, tokens, width), jnp.float32),
            pltpu.VMEM((tokens, LANES), jnp.float32),
            pltpu.VMEM((tokens, LANES), jnp.int32),
        ],
        compiler_params=params(),
        cost_estimate=pl.CostEstimate(
            flops=2 * tokens * depth * features,
            bytes_accessed=2 * depth * (features + tokens),
            transcendentals=0,
        ),
    )(resid, weight, bias, slot_index)


def spread_kernel(top_ref, deep_ref, place_ref, index_ref, value_ref, *refs):
    out_ref = refs[-1]
    place = place_ref[pl.program_id(0)]
    blocks = index_ref.shape[1]
    features = out_ref.shape[2]
    groups = features // LANES
    top = top_ref[0]
    source = jnp.bitwise_xor(top, place)
    span = ROWS * SLOTS

    def rows_of(block, rounds):
        high = lax.broadcasted_iota(jnp.int32, (groups * ROWS, span), 0)
        low = lax.broadcasted_iota(jnp.int32, (LANES, span), 0)
        token = lax.broadcasted_iota(jnp.int32, (1, span), 1) // SLOTS
        total = None
        for turn in range(rounds):
            at = pl.ds(turn * span, span)
            index = index_ref[0, pl.ds(block, 1), at]
            value = value_ref[0, pl.ds(block, 1), at]
            key = (index >> 7) * ROWS + token
            lane = index & (LANES - 1)
            left = jnp.where(
                jnp.broadcast_to(key, high.shape) == high, jnp.broadcast_to(value, high.shape), 0.0
            ).astype(jnp.bfloat16)
            right = jnp.where(jnp.broadcast_to(lane, low.shape) == low, 1.0, 0.0).astype(
                jnp.bfloat16
            )
            part = lax.dot_general(
                left, right, (((1,), (1,)), ((), ())), preferred_element_type=jnp.float32
            )
            total = part if total is None else total + part
        return total

    def run(rounds, unroll):
        def pair(i, carry):
            one, two = rows_of(2 * i, rounds), rows_of(2 * i + 1, rounds)
            rows = pl.ds(pl.multiple_of(i * 2 * ROWS, 2 * ROWS), 2 * ROWS)
            for group in range(groups):
                part = slice(group * ROWS, (group + 1) * ROWS)
                out_ref[0, rows, group * LANES : (group + 1) * LANES] = jnp.concatenate(
                    [one[part], two[part]], axis=0
                ).astype(out_ref.dtype)
            return carry

        lax.fori_loop(0, blocks // 2, pair, 0, unroll=unroll)

    deep = deep_ref[pl.program_id(0)]

    @pl.when((source <= top) & (deep == 0))
    def _():
        run(1, 8)

    @pl.when((source <= top) & (deep != 0))
    def _():
        run(index_ref.shape[2] // span, 1)


def spread(top, places, index, value, features, layers, held=None):
    count, blocks, wide = index.shape
    block = min(32, blocks)
    deep = jnp.any(index[:, :, ROWS * SLOTS :] != FAR, axis=(1, 2)).astype(jnp.int32)
    operands = [top, deep, jnp.array(places, jnp.int32), index, value]
    in_specs = [pl.BlockSpec((1, block, wide), lambda p, b, top, deep, place: (p, b, 0))] * 2
    aliases = {}
    if held is not None:
        operands.append(held)
        in_specs = in_specs + [pl.BlockSpec(memory_space=pl.ANY)]
        aliases = {5: 0}
    tokens = blocks * ROWS
    return pl.pallas_call(
        spread_kernel,
        grid_spec=pltpu.PrefetchScalarGridSpec(
            num_scalar_prefetch=3,
            grid=(count, blocks // block),
            in_specs=in_specs,
            out_specs=pl.BlockSpec(
                (1, block * ROWS, features),
                lambda p, b, top, deep, place: (jnp.bitwise_xor(top[0], place[p]), b, 0),
            ),
        ),
        out_shape=jax.ShapeDtypeStruct((layers, tokens, features), jnp.bfloat16),
        input_output_aliases=aliases,
        compiler_params=params(),
        cost_estimate=pl.CostEstimate(
            flops=count * 2 * tokens * features * 1000,
            bytes_accessed=count * tokens * features * 2,
            transcendentals=0,
        ),
    )(*operands)


def relative_block(me, place, bits):
    pattern = sum(((place >> j) & 1) << (bits - 1 - j) for j in range(bits))
    return jnp.bitwise_xor(me, pattern)


def rebuild_kernel(bits, top_ref, me_ref, value_ref, weight_ref, after_ref, *refs):
    keep_refs, send_refs, total_ref = refs[: len(refs) // 2], refs[len(refs) // 2 : -1], refs[-1]
    source = pl.program_id(0)

    @pl.when(source == 0)
    def _():
        total_ref[...] = jnp.dot(value_ref[0], weight_ref[0], preferred_element_type=jnp.float32)

    @pl.when((source > 0) & (source <= top_ref[0]))
    def _():
        total_ref[...] += jnp.dot(value_ref[0], weight_ref[0], preferred_element_type=jnp.float32)

    @pl.when(source == pl.num_programs(0) - 1)
    def _():
        count = 1 << bits
        rows = total_ref.shape[0] // count
        half = count // 2
        width = keep_refs[0].shape[1]
        for place in range(count):
            start = pl.multiple_of(relative_block(me_ref[0], place, bits) * rows, rows)
            for piece in range(len(keep_refs)):
                block = total_ref[pl.ds(start, rows), piece * width : (piece + 1) * width]
                if place < half:
                    keep_refs[piece][place * rows : (place + 1) * rows, :] = block
                else:
                    at = (place - half) * rows
                    send_refs[piece][at : at + rows, :] = block.astype(jnp.bfloat16)


def rebuild(top, me, values, weight, start, width, piece, bits, after):
    layers, tokens, features = values.shape
    first = start // width
    pieces = width // piece
    shape = (tokens // 2, piece)
    outs = pl.pallas_call(
        functools.partial(rebuild_kernel, bits),
        grid_spec=pltpu.PrefetchScalarGridSpec(
            num_scalar_prefetch=2,
            grid=(layers,),
            in_specs=[
                pl.BlockSpec(
                    (1, tokens, features), lambda s, top, me: (jnp.minimum(s, top[0]), 0, 0)
                ),
                pl.BlockSpec(
                    (1, features, width), lambda s, top, me: (jnp.minimum(s, top[0]), 0, first)
                ),
                pl.BlockSpec(memory_space=pl.ANY),
            ],
            out_specs=[pl.BlockSpec(shape, lambda s, top, me: (0, 0))] * (2 * pieces),
            scratch_shapes=[pltpu.VMEM((tokens, width), jnp.float32)],
        ),
        out_shape=[jax.ShapeDtypeStruct(shape, jnp.float32)] * pieces
        + [jax.ShapeDtypeStruct(shape, jnp.bfloat16)] * pieces,
        compiler_params=params(),
        cost_estimate=pl.CostEstimate(
            flops=2 * layers * tokens * features * width,
            bytes_accessed=2 * layers * features * (tokens + width),
            transcendentals=0,
        ),
    )(top, me, values, weight, after)
    return list(zip(outs[:pieces], outs[pieces:]))


def grad_kernel(bits, pieces, top_ref, me_ref, value_ref, *refs):
    near_refs, far_refs = refs[:pieces], refs[pieces : 2 * pieces]
    out_ref, error_ref = refs[-2:]
    source = pl.program_id(0)

    @pl.when(source == 0)
    def _():
        count = 1 << bits
        rows = error_ref.shape[0] // count
        half = count // 2
        width = near_refs[0].shape[1]
        for place in range(count):
            start = pl.multiple_of(relative_block(me_ref[0], place, bits) * rows, rows)
            for piece in range(pieces):
                from_ref = near_refs[piece] if place < half else far_refs[piece]
                at = (place % half) * rows
                error_ref[pl.ds(start, rows), piece * width : (piece + 1) * width] = from_ref[
                    at : at + rows, :
                ]

    @pl.when(source <= top_ref[0])
    def _():
        out_ref[0] = lax.dot_general(
            value_ref[0],
            error_ref[...],
            (((0,), (0,)), ((), ())),
            preferred_element_type=jnp.float32,
        ).astype(out_ref.dtype)

    @pl.when(source > top_ref[0])
    def _():
        out_ref[...] = jnp.zeros_like(out_ref)


def gradients(top, me, values, halves, start, width, depth, bits, held, after):
    layers, tokens, features = values.shape
    pieces = len(halves)
    piece = width // pieces
    first = start // width
    operands = [top, me, values] + [near for near, _ in halves] + [far for _, far in halves]
    in_specs = [
        pl.BlockSpec((1, tokens, features), lambda s, top, me: (jnp.minimum(s, top[0]), 0, 0))
    ] + [pl.BlockSpec((tokens // 2, piece), lambda s, top, me: (0, 0))] * (2 * pieces)
    operands.append(after)
    in_specs.append(pl.BlockSpec(memory_space=pl.ANY))
    aliases = {}
    if held is not None:
        aliases = {len(operands): 0}
        operands.append(held)
        in_specs.append(pl.BlockSpec(memory_space=pl.ANY))
    return pl.pallas_call(
        functools.partial(grad_kernel, bits, pieces),
        grid_spec=pltpu.PrefetchScalarGridSpec(
            num_scalar_prefetch=2,
            grid=(layers,),
            in_specs=in_specs,
            out_specs=pl.BlockSpec((1, features, width), lambda s, top, me: (s, 0, first)),
            scratch_shapes=[pltpu.VMEM((tokens, width), jnp.bfloat16)],
        ),
        out_shape=jax.ShapeDtypeStruct((layers, features, depth), jnp.bfloat16),
        input_output_aliases=aliases,
        compiler_params=params(),
        cost_estimate=pl.CostEstimate(
            flops=2 * layers * tokens * features * width,
            bytes_accessed=2 * layers * features * (tokens + width),
            transcendentals=0,
        ),
    )(*operands)


def ordered(kernel, operands, specs, out_shape, after):
    def run(*refs):
        kernel(*refs[: len(operands)], *refs[len(operands) + 1 :])

    return pl.pallas_call(
        run,
        grid=(1,),
        in_specs=specs + [pl.BlockSpec(memory_space=pl.ANY)],
        out_specs=[pl.BlockSpec(x.shape, lambda i: (0, 0)) for x in out_shape],
        out_shape=out_shape,
        compiler_params=params(SMALL_BYTES),
        cost_estimate=pl.CostEstimate(flops=1000, bytes_accessed=1 << 20, transcendentals=0),
    )(*operands, after)


def columns_of(x, width, at):
    return pl.BlockSpec((x.shape[0], width), lambda i: (0, at))


def split(keep, arrived, width, at, after):
    rows = keep.shape[0] // 2

    def kernel(keep_ref, arrived_ref, out_ref, send_ref):
        out_ref[...] = keep_ref[:rows, :] + arrived_ref[:rows, :].astype(jnp.float32)
        send_ref[...] = (keep_ref[rows:, :] + arrived_ref[rows:, :].astype(jnp.float32)).astype(
            send_ref.dtype
        )

    return ordered(
        kernel,
        [keep, arrived],
        [columns_of(keep, width, at), columns_of(arrived, width, at)],
        [
            jax.ShapeDtypeStruct((rows, width), jnp.float32),
            jax.ShapeDtypeStruct((rows, width), jnp.bfloat16),
        ],
        after,
    )


def error_of(keep, arrived, bias, target, width, at, after):
    rows = keep.shape[0]

    def kernel(keep_ref, arrived_ref, bias_ref, target_ref, error_ref, half_ref):
        total = keep_ref[...] + arrived_ref[...].astype(jnp.float32)
        error = total + bias_ref[...] - target_ref[...].astype(jnp.float32)
        error_ref[...] = error
        half_ref[...] = error.astype(half_ref.dtype)

    return ordered(
        kernel,
        [keep, arrived, bias, target],
        [
            columns_of(keep, width, 0),
            columns_of(arrived, width, 0),
            columns_of(bias, width, at),
            columns_of(target, width, at),
        ],
        [
            jax.ShapeDtypeStruct((rows, width), jnp.float32),
            jax.ShapeDtypeStruct((rows, width), jnp.bfloat16),
        ],
        after,
    )


def joined(pieces, after):
    rows, width = pieces[0][0].shape

    def kernel(*refs):
        out_ref = refs[-1]
        for i in range(len(pieces)):
            columns = slice(i * width, (i + 1) * width)
            out_ref[:rows, columns] = refs[2 * i][...]
            out_ref[rows:, columns] = refs[2 * i + 1][...]

    operands = [x for piece in pieces for x in piece]
    return ordered(
        kernel,
        operands,
        [columns_of(x, width, 0) for x in operands],
        [jax.ShapeDtypeStruct((2 * rows, width * len(pieces)), jnp.bfloat16)],
        after,
    )[0]


def local(resid, enc_weight, enc_bias, active, dec_weight, dec_bias, target):
    features = enc_weight.shape[2]
    layers = dec_weight.shape[1]
    tokens, depth = resid.shape[1:]
    slots = active.shape[2]
    shards = lax.axis_size("feat")
    bits = shards.bit_length() - 1
    rows = tokens // shards
    feat_index = lax.axis_index("feat")
    pair_index = lax.axis_index("pair")
    top = pair_index.astype(jnp.int32).reshape(1)
    me = feat_index.astype(jnp.int32).reshape(1)

    offset = active[0] - feat_index * features
    inside = (offset >= 0) & (offset < features)
    slot_index = jnp.sort(jnp.where(inside, offset, FAR), axis=1)

    def folded(x):
        x = x.reshape(tokens // ROWS, ROWS, slots // SLOTS, SLOTS)
        return x.transpose(0, 2, 1, 3).reshape(tokens // ROWS, ROWS * slots)

    def across(x, step):
        return lax.ppermute(x, "pair", [(i, i ^ step) for i in range(layers)])

    far_step, near_step = layers // 2, 1
    own_index = folded(slot_index)
    own_short = own_index.astype(jnp.int16)
    far_short = across(own_short, far_step)
    own_value = folded(encode(resid[0], enc_weight[0], enc_bias, slot_index))
    far_value = across(own_value, far_step)

    def pack(*xs):
        return jnp.stack(xs)

    def wide(x):
        return x.astype(jnp.float32 if x.dtype == jnp.bfloat16 else jnp.int32)

    values = spread(top, (0,), own_index[None], wide(own_value)[None], features, layers)
    near_short = across(pack(own_short, far_short), near_step)
    near_value = across(pack(own_value, far_value), near_step)
    values = spread(
        top, (far_step,), wide(far_short)[None], wide(far_value)[None], features, layers, values
    )
    values = spread(
        top,
        (near_step, near_step + far_step),
        wide(near_short),
        wide(near_value),
        features,
        layers,
        values,
    )

    def swap(x, bit):
        return lax.ppermute(x, "feat", [(i, i ^ (1 << bit)) for i in range(shards)])

    piece = min(PIECE, depth)
    chunk = min(CHUNK, depth)
    per = chunk // piece
    last = values

    class Chunk:
        pass

    chunks = []
    for start in range(0, depth, chunk):
        c = Chunk()
        c.start = start
        ((keep, send),) = rebuild(top, me, values, dec_weight[0], start, chunk, chunk, bits, last)
        last = send
        c.state = [(keep, swap(send, 0), i) for i in range(per)]
        chunks.append(c)

    def reduce_step(c, bit):
        nonlocal last
        for i, (keep, arrived, at) in enumerate(c.state):
            keep, send = split(keep, arrived, piece, at, last)
            last = send
            c.state[i] = (keep, swap(send, bit), 0)

    def error_step(c):
        nonlocal last
        c.errors = []
        for i, (keep, arrived, _) in enumerate(c.state):
            error, near = error_of(
                keep, arrived, dec_bias, target[0], piece, c.start // piece + i, last
            )
            last = near
            c.errors.append(error)
            c.state[i] = (near, swap(near, bits - 1))

    def gather_step(c, bit):
        nonlocal last
        if bit > 0:
            for i, pair in enumerate(c.state):
                near = joined([pair], last)
                last = near
                c.state[i] = (near, swap(near, bit))
        else:
            near = joined(c.state, last)
            last = near
            c.halves = [(near, swap(near, 0))]

    def first_steps(c):
        return [lambda: reduce_step(c, 1)]

    def later_steps(c):
        steps = [lambda bit=bit: reduce_step(c, bit) for bit in range(2, bits)]
        steps.append(lambda: error_step(c))
        steps += [lambda bit=bit: gather_step(c, bit) for bit in reversed(range(bits - 1))]
        return steps

    plan = first_steps(chunks[0]) + later_steps(chunks[0])
    for c in chunks[1:]:
        plan = plan[:-1] + first_steps(c) + plan[-1:] + later_steps(c)
    for step in plan:
        step()
    grads = None
    for c in chunks:
        grads = gradients(
            top, me, values, c.halves, c.start, chunk, depth, bits, grads, last
        )
    error = jnp.concatenate([error for c in chunks for error in c.errors], axis=1)
    return (error[None], grads[None])


def solution(mesh):
    in_specs = (
        P("pair", None, None),
        P("pair", None, "feat"),
        P("pair", "feat"),
        P("pair", None, None),
        P("pair", None, "feat", None),
        P("pair", None),
        P("pair", "feat", None),
    )
    out_specs = (P("pair", "feat", None), P("pair", None, "feat", None))
    return jax.shard_map(local, mesh=mesh, in_specs=in_specs, out_specs=out_specs, check_vma=False)
```

```python
import functools

import jax
import jax.numpy as jnp
from jax import lax
from jax.experimental import pallas as pl
from jax.experimental.pallas import tpu as pltpu
from jax.sharding import PartitionSpec as P

LANES = 128
ROWS = 8
SLOTS = 32
FAR = 32767
ENCODE_BYTES = 56 * 1024 * 1024
VMEM_BYTES = 24 * 1024 * 1024
SMALL_BYTES = 8 * 1024 * 1024
PIECE = 512
GROUPS = (
    (((1,), (2,)), ((2,), (1,))),
    (((1,), (2,)), ((2,), (1,))),
    (((1,), (2,)), ((2,), (1,))),
    (((1,), (2,)), ((2,), (1,))),
)
REBUILD, GRADIENT = -1, -2
PLAN = (
    (0, REBUILD), (1, REBUILD), (0, 0), (2, REBUILD), (0, 1), (1, 0), (3, REBUILD), (0, 2), (1, 1),
    (2, 0), (0, 3), (1, 2), (2, 1), (0, 4), (3, 0), (1, 3), (2, 2), (3, 1), (1, 4), (2, 3), (3, 2),
    (0, GRADIENT), (2, 4), (3, 3), (1, GRADIENT), (3, 4), (2, GRADIENT), (3, GRADIENT),
)


WHOLE = pl.BlockSpec(memory_space=pltpu.VMEM)


def in_vmem(x):
    return pltpu.with_memory_space_constraint(x, pltpu.VMEM)


def params(limit=VMEM_BYTES):
    return pltpu.CompilerParams(vmem_limit_bytes=limit)


def encode_kernel(resid_ref, weight_ref, bias_ref, slot_ref, out_ref, pre_ref, picked_ref, index_ref):
    step = pl.program_id(0)
    tokens = resid_ref.shape[0]
    width = weight_ref.shape[1]
    slots = slot_ref.shape[1]
    groups = width // LANES

    @pl.when(step == 0)
    def _():
        picked_ref[...] = jnp.zeros_like(picked_ref)
        pre_ref[1] = jnp.zeros_like(pre_ref[1])
        index_ref[...] = jnp.full_like(index_ref, FAR)
        index_ref[:, :slots] = slot_ref[...]

    now = lax.rem(step, 2)
    before = 1 - now
    first = (step - 1) * groups

    def pick():
        for row in range(0, tokens, ROWS):
            rows = pl.ds(row, ROWS)
            index = index_ref[rows, :]
            group = (index >> 7) - first
            lane = index & (LANES - 1)
            picked = picked_ref[rows, :]
            for part in range(groups):
                source = pre_ref[before, rows, part * LANES : (part + 1) * LANES]
                found = jnp.take_along_axis(source, lane, axis=1)
                picked = jnp.where(group == part, found, picked)
            picked_ref[rows, :] = picked

    @pl.when(step < pl.num_programs(0) - 1)
    def _():
        pre_ref[now] = (
            jnp.dot(resid_ref[...], weight_ref[...], preferred_element_type=jnp.float32)
            + bias_ref[...]
        )
        pick()

    @pl.when(step == pl.num_programs(0) - 1)
    def _():
        pick()
        out_ref[...] = jnp.maximum(picked_ref[:, :slots], 0.0).astype(out_ref.dtype)


def encode(resid, weight, bias, slot_index):
    tokens, depth = resid.shape
    features = weight.shape[1]
    slots = slot_index.shape[1]
    width = min(256, features)
    steps = features // width
    return pl.pallas_call(
        encode_kernel,
        grid=(steps + 1,),
        in_specs=[
            WHOLE,
            pl.BlockSpec((depth, width), lambda i: (0, jnp.minimum(i, steps - 1))),
            pl.BlockSpec((1, width), lambda i: (0, jnp.minimum(i, steps - 1))),
            pl.BlockSpec((tokens, slots), lambda i: (0, 0)),
        ],
        out_specs=pl.BlockSpec((tokens, slots), lambda i: (0, 0)),
        out_shape=jax.ShapeDtypeStruct((tokens, slots), jnp.bfloat16),
        scratch_shapes=[
            pltpu.VMEM((2, tokens, width), jnp.float32),
            pltpu.VMEM((tokens, LANES), jnp.float32),
            pltpu.VMEM((tokens, LANES), jnp.int32),
        ],
        compiler_params=params(ENCODE_BYTES),
        cost_estimate=pl.CostEstimate(
            flops=2 * tokens * depth * features,
            bytes_accessed=2 * depth * (features + tokens),
            transcendentals=0,
        ),
    )(in_vmem(resid), weight, bias, slot_index)


def spread_kernel(places, top_ref, deep_ref, index_ref, value_ref, out_ref):
    at = pl.program_id(0)
    place = places[0] + at * (places[-1] - places[0])
    blocks = index_ref.shape[1]
    features = out_ref.shape[2]
    groups = features // LANES
    top = top_ref[0]
    source = jnp.bitwise_xor(top, place)
    span = ROWS * SLOTS

    def rows_of(block, rounds):
        high = lax.broadcasted_iota(jnp.int32, (groups * ROWS, span), 0)
        low = lax.broadcasted_iota(jnp.int32, (LANES, span), 0)
        token = lax.broadcasted_iota(jnp.int32, (1, span), 1) // SLOTS
        total = None
        for turn in range(rounds):
            part = pl.ds(turn * span, span)
            index = index_ref[0, pl.ds(block, 1), part]
            value = value_ref[0, pl.ds(block, 1), part]
            key = (index >> 7) * ROWS + token
            lane = index & (LANES - 1)
            left = jnp.where(
                jnp.broadcast_to(key, high.shape) == high, jnp.broadcast_to(value, high.shape), 0.0
            ).astype(jnp.bfloat16)
            right = jnp.where(jnp.broadcast_to(lane, low.shape) == low, 1.0, 0.0).astype(
                jnp.bfloat16
            )
            part = lax.dot_general(
                left, right, (((1,), (1,)), ((), ())), preferred_element_type=jnp.float32
            )
            total = part if total is None else total + part
        return total

    def run(rounds, unroll):
        def pair(i, carry):
            one, two = rows_of(2 * i, rounds), rows_of(2 * i + 1, rounds)
            first = (pl.program_id(1) * blocks + 2 * i) * ROWS
            rows = pl.ds(pl.multiple_of(first, 2 * ROWS), 2 * ROWS)
            for group in range(groups):
                part = slice(group * ROWS, (group + 1) * ROWS)
                out_ref[at, rows, group * LANES : (group + 1) * LANES] = jnp.concatenate(
                    [one[part], two[part]], axis=0
                ).astype(out_ref.dtype)
            return carry

        lax.fori_loop(0, blocks // 2, pair, 0, unroll=unroll)

    deep = deep_ref[at]

    @pl.when((source <= top) & (deep == 0))
    def _():
        run(1, 8)

    @pl.when((source <= top) & (deep != 0))
    def _():
        run(index_ref.shape[2] // span, 1)


def spread(top, places, index, value, features):
    count, blocks, wide = index.shape
    block = min(32, blocks)
    deep = jnp.any(index[:, :, ROWS * SLOTS :] != FAR, axis=(1, 2)).astype(jnp.int32)
    tokens = blocks * ROWS
    return pl.pallas_call(
        functools.partial(spread_kernel, places),
        grid_spec=pltpu.PrefetchScalarGridSpec(
            num_scalar_prefetch=2,
            grid=(count, blocks // block),
            in_specs=[pl.BlockSpec((1, block, wide), lambda p, b, top, deep: (p, b, 0))] * 2,
            out_specs=WHOLE,
        ),
        out_shape=pltpu.VMEM((count, tokens, features), jnp.bfloat16),
        compiler_params=params(),
        cost_estimate=pl.CostEstimate(
            flops=count * 2 * tokens * features * 1000,
            bytes_accessed=count * tokens * features * 2,
            transcendentals=0,
        ),
    )(top, deep, index, value)


PLACES = (0, 2, 1, 3)


def layer_at(top, step):
    place = jnp.where(step == 0, 0, jnp.where(step == 1, PLACES[1], 2 * step - 3))
    return jnp.bitwise_xor(top, place)


def each_layer(top, value_refs, body, otherwise):
    own_ref, far_ref, near_ref = value_refs
    step = pl.program_id(0)
    used = layer_at(top, step) <= top

    @pl.when(step == 0)
    def _():
        body(own_ref.at[0], True)

    @pl.when((step == 1) & used)
    def _():
        body(far_ref.at[0], False)

    @pl.when((step > 1) & used)
    def _():
        body(near_ref.at[step - 2], False)

    if otherwise is not None:
        pl.when(jnp.logical_not(used))(otherwise)


def relative_block(me, place, bits):
    pattern = sum(((place >> j) & 1) << (bits - 1 - j) for j in range(bits))
    return jnp.bitwise_xor(me, pattern)


def rebuild_kernel(bits, top_ref, me_ref, own_ref, far_ref, near_ref, weight_ref, after_ref, *refs):
    keep_refs, send_refs, total_ref = refs[: len(refs) // 2], refs[len(refs) // 2 : -1], refs[-1]
    step = pl.program_id(0)

    def add(value_ref, first):
        product = jnp.dot(value_ref[...], weight_ref[0], preferred_element_type=jnp.float32)
        total_ref[...] = product if first else total_ref[...] + product

    each_layer(top_ref[0], (own_ref, far_ref, near_ref), add, None)

    @pl.when(step == pl.num_programs(0) - 1)
    def _():
        count = 1 << bits
        rows = total_ref.shape[0] // count
        half = count // 2
        width = keep_refs[0].shape[1]
        for place in range(count):
            start = pl.multiple_of(relative_block(me_ref[0], place, bits) * rows, rows)
            for piece in range(len(keep_refs)):
                block = total_ref[pl.ds(start, rows), piece * width : (piece + 1) * width]
                if place < half:
                    keep_refs[piece][place * rows : (place + 1) * rows, :] = block
                else:
                    at = (place - half) * rows
                    send_refs[piece][at : at + rows, :] = block.astype(jnp.bfloat16)


def rebuild(top, me, values, weight, start, width, piece, bits, after):
    layers = weight.shape[0]
    tokens, features = values[0].shape[1:]
    first = start // width
    pieces = width // piece
    shape = (tokens // 2, piece)
    outs = pl.pallas_call(
        functools.partial(rebuild_kernel, bits),
        grid_spec=pltpu.PrefetchScalarGridSpec(
            num_scalar_prefetch=2,
            grid=(layers,),
            in_specs=[
                WHOLE,
                WHOLE,
                WHOLE,
                pl.BlockSpec(
                    (1, features, width),
                    lambda s, top, me: (jnp.minimum(layer_at(top[0], s), top[0]), 0, first),
                ),
                pl.BlockSpec(memory_space=pl.ANY),
            ],
            out_specs=[pl.BlockSpec(shape, lambda s, top, me: (0, 0))] * (2 * pieces),
            scratch_shapes=[pltpu.VMEM((tokens, width), jnp.float32)],
        ),
        out_shape=[jax.ShapeDtypeStruct(shape, jnp.float32)] * pieces
        + [jax.ShapeDtypeStruct(shape, jnp.bfloat16)] * pieces,
        compiler_params=params(),
        cost_estimate=pl.CostEstimate(
            flops=2 * layers * tokens * features * width,
            bytes_accessed=2 * layers * features * (tokens + width),
            transcendentals=0,
        ),
    )(top, me, *map(in_vmem, values), weight, after)
    return list(zip(outs[:pieces], outs[pieces:]))


def grad_kernel(bits, pieces, top_ref, me_ref, own_ref, far_ref, near_ref, *refs):
    near_refs, far_refs = refs[:pieces], refs[pieces : 2 * pieces]
    out_ref, done_ref, error_ref = refs[-3:]
    source = pl.program_id(0)

    @pl.when(source == 0)
    def _():
        done_ref[...] = jnp.zeros_like(done_ref)
        count = 1 << bits
        rows = error_ref.shape[0] // count
        half = count // 2
        width = near_refs[0].shape[1]
        for place in range(count):
            start = pl.multiple_of(relative_block(me_ref[0], place, bits) * rows, rows)
            for piece in range(pieces):
                from_ref = near_refs[piece] if place < half else far_refs[piece]
                at = (place % half) * rows
                error_ref[pl.ds(start, rows), piece * width : (piece + 1) * width] = from_ref[
                    at : at + rows, :
                ]

    def multiply(value_ref, first):
        out_ref[0] = lax.dot_general(
            value_ref[...],
            error_ref[...],
            (((0,), (0,)), ((), ())),
            preferred_element_type=jnp.float32,
        ).astype(out_ref.dtype)

    def clear():
        out_ref[...] = jnp.zeros_like(out_ref)

    each_layer(top_ref[0], (own_ref, far_ref, near_ref), multiply, clear)


def gradients(top, me, values, halves, start, width, depth, bits, held, after):
    layers = sum(x.shape[0] for x in values)
    tokens, features = values[0].shape[1:]
    pieces = len(halves)
    piece = width // pieces
    first = start // width
    operands = [top, me, *map(in_vmem, values)] + [near for near, _ in halves] + [far for _, far in halves]
    in_specs = [WHOLE] * 3 + [pl.BlockSpec((tokens // 2, piece), lambda s, top, me: (0, 0))] * (2 * pieces)
    operands.append(after)
    in_specs.append(pl.BlockSpec(memory_space=pl.ANY))
    aliases = {}
    if held is not None:
        aliases = {len(operands): 0}
        operands.append(held)
        in_specs.append(pl.BlockSpec(memory_space=pl.ANY))
    return pl.pallas_call(
        functools.partial(grad_kernel, bits, pieces),
        grid_spec=pltpu.PrefetchScalarGridSpec(
            num_scalar_prefetch=2,
            grid=(layers,),
            in_specs=in_specs,
            out_specs=[
                pl.BlockSpec(
                    (1, features, width), lambda s, top, me: (layer_at(top[0], s), 0, first)
                ),
                pl.BlockSpec((ROWS, LANES), lambda s, top, me: (0, 0)),
            ],
            scratch_shapes=[pltpu.VMEM((tokens, width), jnp.bfloat16)],
        ),
        out_shape=[
            jax.ShapeDtypeStruct((layers, features, depth), jnp.bfloat16),
            jax.ShapeDtypeStruct((ROWS, LANES), jnp.float32),
        ],
        input_output_aliases=aliases,
        compiler_params=params(),
        cost_estimate=pl.CostEstimate(
            flops=2 * layers * tokens * features * width,
            bytes_accessed=2 * layers * features * (tokens + width),
            transcendentals=0,
        ),
    )(*operands)


def ordered(kernel, operands, specs, out_shape, after):
    def run(*refs):
        kernel(*refs[: len(operands)], *refs[len(operands) + 1 :])

    return pl.pallas_call(
        run,
        grid=(1,),
        in_specs=specs + [pl.BlockSpec(memory_space=pl.ANY)],
        out_specs=[pl.BlockSpec(x.shape, lambda i: (0, 0)) for x in out_shape],
        out_shape=out_shape,
        compiler_params=params(SMALL_BYTES),
        cost_estimate=pl.CostEstimate(flops=1000, bytes_accessed=1 << 20, transcendentals=0),
    )(*operands, after)


def columns_of(x, width, at):
    return pl.BlockSpec((x.shape[0], width), lambda i: (0, at))


def split(keep, arrived, parts, after):
    rows, width = keep.shape[0] // parts, keep.shape[1]

    def kernel(*refs):
        keep_ref, arrived_refs = refs[0], refs[1 : 1 + len(arrived)]
        for part, out_ref in enumerate(refs[1 + len(arrived) :]):
            at = slice(part * rows, (part + 1) * rows)
            total = keep_ref[at, :]
            for arrived_ref in arrived_refs:
                total = total + arrived_ref[at, :].astype(jnp.float32)
            out_ref[...] = total.astype(out_ref.dtype)

    operands = [keep, *arrived]
    outs = ordered(
        kernel,
        operands,
        [columns_of(x, width, 0) for x in operands],
        [jax.ShapeDtypeStruct((rows, width), jnp.float32)]
        + [jax.ShapeDtypeStruct((rows, width), jnp.bfloat16)] * (parts - 1),
        after,
    )
    return outs[0], outs[1:]


def error_of(keep, arrived, bias, target, at, after):
    rows, width = keep.shape

    def kernel(bias_ref, target_ref, keep_ref, *refs):
        total = keep_ref[...]
        for arrived_ref in refs[:-2]:
            total = total + arrived_ref[...].astype(jnp.float32)
        error = total + bias_ref[...] - target_ref[...].astype(jnp.float32)
        refs[-2][...] = error
        refs[-1][...] = error.astype(jnp.bfloat16)

    return ordered(
        kernel,
        [bias, target, keep, *arrived],
        [columns_of(bias, width, at), columns_of(target, width, at)]
        + [columns_of(x, width, 0) for x in [keep, *arrived]],
        [
            jax.ShapeDtypeStruct((rows, width), jnp.float32),
            jax.ShapeDtypeStruct((rows, width), jnp.bfloat16),
        ],
        after,
    )


def joined(arrays, after):
    rows, width = arrays[0].shape

    def kernel(*refs):
        for i, ref in enumerate(refs[:-1]):
            refs[-1][i * rows : (i + 1) * rows, :] = ref[...]

    return ordered(
        kernel,
        arrays,
        [columns_of(x, width, 0) for x in arrays],
        [jax.ShapeDtypeStruct((rows * len(arrays), width), jnp.bfloat16)],
        after,
    )[0]


def local(resid, enc_weight, enc_bias, active, dec_weight, dec_bias, target):
    features = enc_weight.shape[2]
    layers = dec_weight.shape[1]
    tokens, depth = resid.shape[1:]
    slots = active.shape[2]
    shards = lax.axis_size("feat")
    bits = shards.bit_length() - 1
    rows = tokens // shards
    feat_index = lax.axis_index("feat")
    pair_index = lax.axis_index("pair")
    top = pair_index.astype(jnp.int32).reshape(1)
    me = feat_index.astype(jnp.int32).reshape(1)

    offset = active[0] - feat_index * features
    inside = (offset >= 0) & (offset < features)
    slot_index = jnp.sort(jnp.where(inside, offset, FAR), axis=1)

    def folded(x):
        x = x.reshape(tokens // ROWS, ROWS, slots // SLOTS, SLOTS)
        return x.transpose(0, 2, 1, 3).reshape(tokens // ROWS, ROWS * slots)

    def across(x, step):
        return lax.ppermute(x, "pair", [(i, i ^ step) for i in range(layers)])

    far_step, near_step = layers // 2, 1
    own_index = folded(slot_index)
    own_short = own_index.astype(jnp.int16)
    far_short = across(own_short, far_step)
    own_value = folded(encode(resid[0], enc_weight[0], enc_bias, slot_index))
    far_value = across(own_value, far_step)

    def pack(*xs):
        return jnp.stack(xs)

    def wide(x):
        return x.astype(jnp.float32 if x.dtype == jnp.bfloat16 else jnp.int32)

    own = spread(top, (0,), own_index[None], wide(own_value)[None], features)
    near_short = across(pack(own_short, far_short), near_step)
    near_value = across(pack(own_value, far_value), near_step)
    far = spread(top, (far_step,), wide(far_short)[None], wide(far_value)[None], features)
    near = spread(
        top, (near_step, near_step + far_step), wide(near_short), wide(near_value), features
    )
    values = (own, far, near)

    def swap(parts, group):
        masks = [
            sum(((part >> j) & 1) << group[-1 - j] for j in range(len(group)))
            for part in range(1, 1 << len(group))
        ]
        return [
            lax.ppermute(x, "feat", [(i, i ^ mask) for i in range(shards)])
            for x, mask in zip(parts, masks)
        ]

    piece = min(PIECE, depth)
    count = depth // piece
    last = top
    grads = None
    state = [None] * count
    halves = [None] * count
    errors = [None] * count

    def rebuild_step(p):
        nonlocal last
        ((keep, last),) = rebuild(
            top, me, values, dec_weight[0], p * piece, piece, piece, bits, last
        )
        state[p] = (keep, swap([last], (0,)))

    def reduce_step(p, group):
        nonlocal last
        keep, sends = split(*state[p], 1 << len(group), last)
        last = sends[-1]
        state[p] = (keep, swap(sends, group))

    def error_step(p, group):
        nonlocal last
        errors[p], last = error_of(*state[p], dec_bias, target[0], p, last)
        state[p] = (last, swap([last] * ((1 << len(group)) - 1), group))

    def gather_step(p, group):
        nonlocal last
        last = joined([state[p][0], *state[p][1]], last)
        state[p] = (last, swap([last] * ((1 << len(group)) - 1), group))

    def grad_step(p):
        nonlocal grads, last
        near, (far,) = state[p]
        grads, last = gradients(
            top, me, values, [(near, far)], p * piece, piece, depth, bits, grads, last
        )

    def steps_of(p, down, up):
        steps = [functools.partial(reduce_step, p, group) for group in down]
        steps.append(functools.partial(error_step, p, up[0]))
        steps += [functools.partial(gather_step, p, group) for group in [*up[1:], (0,)]]
        return steps

    if count == len(GROUPS) and bits == 3:
        groups = GROUPS
        plan = PLAN
    else:
        ones = [(bit,) for bit in range(1, bits)]
        groups = [(ones, ones[::-1])] * count
        plan = [(p, REBUILD) for p in range(count)]
        plan += [(p, i) for i in range(2 * bits - 1) for p in range(count)]
        plan += [(p, GRADIENT) for p in range(count)]
    steps = [steps_of(p, *groups[p]) for p in range(count)]
    for p, i in plan:
        if i == REBUILD:
            rebuild_step(p)
        elif i == GRADIENT:
            grad_step(p)
        else:
            steps[p][i]()
    error = jnp.concatenate(errors, axis=1)
    return (error[None], grads[None])


def solution(mesh):
    in_specs = (
        P("pair", None, None),
        P("pair", None, "feat"),
        P("pair", "feat"),
        P("pair", None, None),
        P("pair", None, "feat", None),
        P("pair", None),
        P("pair", "feat", None),
    )
    out_specs = (P("pair", "feat", None), P("pair", None, "feat", None))
    return jax.shard_map(local, mesh=mesh, in_specs=in_specs, out_specs=out_specs, check_vma=False)
```

```python
import functools

import jax
import jax.numpy as jnp
from jax import lax
from jax.experimental import pallas as pl
from jax.experimental.pallas import tpu as pltpu
from jax.sharding import PartitionSpec as P

LANES = 128
ROWS = 8
SLOTS = 32
FAR = 32767
ENCODE_BYTES = 56 * 1024 * 1024
VMEM_BYTES = 24 * 1024 * 1024
SMALL_BYTES = 8 * 1024 * 1024
PIECE = 512
GROUPS = (
    (((1, 2),), ((2,), (1,))),
    (((1,), (2,)), ((2,), (1,))),
    (((1,), (2,)), ((2,), (1,))),
    (((1,), (2,)), ((2,), (1,))),
)
REBUILD, GRADIENT = -1, -2
PLAN = (
    (0, REBUILD), (1, REBUILD), (0, 0), (2, REBUILD), (0, 1), (1, 0), (3, REBUILD), (0, 2), (1, 1),
    (2, 0), (0, 3), (1, 2), (2, 1), (3, 0), (1, 3), (2, 2), (3, 1), (1, 4), (2, 3), (3, 2),
    (0, GRADIENT), (2, 4), (3, 3), (1, GRADIENT), (3, 4), (2, GRADIENT), (3, GRADIENT),
)


WHOLE = pl.BlockSpec(memory_space=pltpu.VMEM)


def in_vmem(x):
    return pltpu.with_memory_space_constraint(x, pltpu.VMEM)


def params(limit=VMEM_BYTES):
    return pltpu.CompilerParams(vmem_limit_bytes=limit)


def encode_kernel(resid_ref, weight_ref, bias_ref, slot_ref, out_ref, pre_ref, picked_ref, index_ref):
    step = pl.program_id(0)
    tokens = resid_ref.shape[0]
    width = weight_ref.shape[1]
    slots = slot_ref.shape[1]
    groups = width // LANES

    @pl.when(step == 0)
    def _():
        picked_ref[...] = jnp.zeros_like(picked_ref)
        pre_ref[1] = jnp.zeros_like(pre_ref[1])
        index_ref[...] = jnp.full_like(index_ref, FAR)
        index_ref[:, :slots] = slot_ref[...]

    now = lax.rem(step, 2)
    before = 1 - now
    first = (step - 1) * groups

    def pick():
        for row in range(0, tokens, ROWS):
            rows = pl.ds(row, ROWS)
            index = index_ref[rows, :]
            group = (index >> 7) - first
            lane = index & (LANES - 1)
            picked = picked_ref[rows, :]
            for part in range(groups):
                source = pre_ref[before, rows, part * LANES : (part + 1) * LANES]
                found = jnp.take_along_axis(source, lane, axis=1)
                picked = jnp.where(group == part, found, picked)
            picked_ref[rows, :] = picked

    @pl.when(step < pl.num_programs(0) - 1)
    def _():
        pre_ref[now] = (
            jnp.dot(resid_ref[...], weight_ref[...], preferred_element_type=jnp.float32)
            + bias_ref[...]
        )
        pick()

    @pl.when(step == pl.num_programs(0) - 1)
    def _():
        pick()
        out_ref[...] = jnp.maximum(picked_ref[:, :slots], 0.0).astype(out_ref.dtype)


def encode(resid, weight, bias, slot_index):
    tokens, depth = resid.shape
    features = weight.shape[1]
    slots = slot_index.shape[1]
    width = min(256, features)
    steps = features // width
    return pl.pallas_call(
        encode_kernel,
        grid=(steps + 1,),
        in_specs=[
            WHOLE,
            pl.BlockSpec((depth, width), lambda i: (0, jnp.minimum(i, steps - 1))),
            pl.BlockSpec((1, width), lambda i: (0, jnp.minimum(i, steps - 1))),
            pl.BlockSpec((tokens, slots), lambda i: (0, 0)),
        ],
        out_specs=pl.BlockSpec((tokens, slots), lambda i: (0, 0)),
        out_shape=jax.ShapeDtypeStruct((tokens, slots), jnp.bfloat16),
        scratch_shapes=[
            pltpu.VMEM((2, tokens, width), jnp.float32),
            pltpu.VMEM((tokens, LANES), jnp.float32),
            pltpu.VMEM((tokens, LANES), jnp.int32),
        ],
        compiler_params=params(ENCODE_BYTES),
        cost_estimate=pl.CostEstimate(
            flops=2 * tokens * depth * features,
            bytes_accessed=2 * depth * (features + tokens),
            transcendentals=0,
        ),
    )(in_vmem(resid), weight, bias, slot_index)


def spread_kernel(places, top_ref, deep_ref, index_ref, value_ref, out_ref):
    at = pl.program_id(0)
    place = places[0] + at * (places[-1] - places[0])
    blocks = index_ref.shape[1]
    features = out_ref.shape[2]
    groups = features // LANES
    top = top_ref[0]
    source = jnp.bitwise_xor(top, place)
    span = ROWS * SLOTS

    def rows_of(block, rounds):
        high = lax.broadcasted_iota(jnp.int32, (groups * ROWS, span), 0)
        low = lax.broadcasted_iota(jnp.int32, (LANES, span), 0)
        token = lax.broadcasted_iota(jnp.int32, (1, span), 1) // SLOTS
        total = None
        for turn in range(rounds):
            part = pl.ds(turn * span, span)
            index = index_ref[0, pl.ds(block, 1), part]
            value = value_ref[0, pl.ds(block, 1), part]
            key = (index >> 7) * ROWS + token
            lane = index & (LANES - 1)
            left = jnp.where(
                jnp.broadcast_to(key, high.shape) == high, jnp.broadcast_to(value, high.shape), 0.0
            ).astype(jnp.bfloat16)
            right = jnp.where(jnp.broadcast_to(lane, low.shape) == low, 1.0, 0.0).astype(
                jnp.bfloat16
            )
            part = lax.dot_general(
                left, right, (((1,), (1,)), ((), ())), preferred_element_type=jnp.float32
            )
            total = part if total is None else total + part
        return total

    def run(rounds, unroll):
        def pair(i, carry):
            one, two = rows_of(2 * i, rounds), rows_of(2 * i + 1, rounds)
            first = (pl.program_id(1) * blocks + 2 * i) * ROWS
            rows = pl.ds(pl.multiple_of(first, 2 * ROWS), 2 * ROWS)
            for group in range(groups):
                part = slice(group * ROWS, (group + 1) * ROWS)
                out_ref[at, rows, group * LANES : (group + 1) * LANES] = jnp.concatenate(
                    [one[part], two[part]], axis=0
                ).astype(out_ref.dtype)
            return carry

        lax.fori_loop(0, blocks // 2, pair, 0, unroll=unroll)

    deep = deep_ref[at]

    @pl.when((source <= top) & (deep == 0))
    def _():
        run(1, 8)

    @pl.when((source <= top) & (deep != 0))
    def _():
        run(index_ref.shape[2] // span, 1)


def spread(top, places, index, value, features):
    count, blocks, wide = index.shape
    block = min(32, blocks)
    deep = jnp.any(index[:, :, ROWS * SLOTS :] != FAR, axis=(1, 2)).astype(jnp.int32)
    tokens = blocks * ROWS
    return pl.pallas_call(
        functools.partial(spread_kernel, places),
        grid_spec=pltpu.PrefetchScalarGridSpec(
            num_scalar_prefetch=2,
            grid=(count, blocks // block),
            in_specs=[pl.BlockSpec((1, block, wide), lambda p, b, top, deep: (p, b, 0))] * 2,
            out_specs=WHOLE,
        ),
        out_shape=pltpu.VMEM((count, tokens, features), jnp.bfloat16),
        compiler_params=params(),
        cost_estimate=pl.CostEstimate(
            flops=count * 2 * tokens * features * 1000,
            bytes_accessed=count * tokens * features * 2,
            transcendentals=0,
        ),
    )(top, deep, index, value)


PLACES = (0, 2, 1, 3)


def layer_at(top, step):
    place = jnp.where(step == 0, 0, jnp.where(step == 1, PLACES[1], 2 * step - 3))
    return jnp.bitwise_xor(top, place)


def each_layer(top, value_refs, body, otherwise):
    own_ref, far_ref, near_ref = value_refs
    step = pl.program_id(0)
    used = layer_at(top, step) <= top

    @pl.when(step == 0)
    def _():
        body(own_ref.at[0], True)

    @pl.when((step == 1) & used)
    def _():
        body(far_ref.at[0], False)

    @pl.when((step > 1) & used)
    def _():
        body(near_ref.at[step - 2], False)

    if otherwise is not None:
        pl.when(jnp.logical_not(used))(otherwise)


def relative_block(me, place, bits):
    pattern = sum(((place >> j) & 1) << (bits - 1 - j) for j in range(bits))
    return jnp.bitwise_xor(me, pattern)


def rebuild_kernel(bits, top_ref, me_ref, own_ref, far_ref, near_ref, weight_ref, after_ref, *refs):
    keep_refs, send_refs, total_ref = refs[: len(refs) // 2], refs[len(refs) // 2 : -1], refs[-1]
    step = pl.program_id(0)

    def add(value_ref, first):
        product = jnp.dot(value_ref[...], weight_ref[0], preferred_element_type=jnp.float32)
        total_ref[...] = product if first else total_ref[...] + product

    each_layer(top_ref[0], (own_ref, far_ref, near_ref), add, None)

    @pl.when(step == pl.num_programs(0) - 1)
    def _():
        count = 1 << bits
        rows = total_ref.shape[0] // count
        half = count // 2
        width = keep_refs[0].shape[1]
        for place in range(count):
            start = pl.multiple_of(relative_block(me_ref[0], place, bits) * rows, rows)
            for piece in range(len(keep_refs)):
                block = total_ref[pl.ds(start, rows), piece * width : (piece + 1) * width]
                if place < half:
                    keep_refs[piece][place * rows : (place + 1) * rows, :] = block
                else:
                    at = (place - half) * rows
                    send_refs[piece][at : at + rows, :] = block.astype(jnp.bfloat16)


def rebuild(top, me, values, weight, start, width, piece, bits, after):
    layers = weight.shape[0]
    tokens, features = values[0].shape[1:]
    first = start // width
    pieces = width // piece
    shape = (tokens // 2, piece)
    outs = pl.pallas_call(
        functools.partial(rebuild_kernel, bits),
        grid_spec=pltpu.PrefetchScalarGridSpec(
            num_scalar_prefetch=2,
            grid=(layers,),
            in_specs=[
                WHOLE,
                WHOLE,
                WHOLE,
                pl.BlockSpec(
                    (1, features, width),
                    lambda s, top, me: (jnp.minimum(layer_at(top[0], s), top[0]), 0, first),
                ),
                pl.BlockSpec(memory_space=pl.ANY),
            ],
            out_specs=[pl.BlockSpec(shape, lambda s, top, me: (0, 0))] * (2 * pieces),
            scratch_shapes=[pltpu.VMEM((tokens, width), jnp.float32)],
        ),
        out_shape=[jax.ShapeDtypeStruct(shape, jnp.float32)] * pieces
        + [jax.ShapeDtypeStruct(shape, jnp.bfloat16)] * pieces,
        compiler_params=params(),
        cost_estimate=pl.CostEstimate(
            flops=2 * layers * tokens * features * width,
            bytes_accessed=2 * layers * features * (tokens + width),
            transcendentals=0,
        ),
    )(top, me, *map(in_vmem, values), weight, after)
    return list(zip(outs[:pieces], outs[pieces:]))


def grad_kernel(bits, pieces, top_ref, me_ref, own_ref, far_ref, near_ref, *refs):
    near_refs, far_refs = refs[:pieces], refs[pieces : 2 * pieces]
    out_ref, done_ref, error_ref = refs[-3:]
    source = pl.program_id(0)

    @pl.when(source == 0)
    def _():
        done_ref[...] = jnp.zeros_like(done_ref)
        count = 1 << bits
        rows = error_ref.shape[0] // count
        half = count // 2
        width = near_refs[0].shape[1]
        for place in range(count):
            start = pl.multiple_of(relative_block(me_ref[0], place, bits) * rows, rows)
            for piece in range(pieces):
                from_ref = near_refs[piece] if place < half else far_refs[piece]
                at = (place % half) * rows
                error_ref[pl.ds(start, rows), piece * width : (piece + 1) * width] = from_ref[
                    at : at + rows, :
                ]

    def multiply(value_ref, first):
        out_ref[0] = lax.dot_general(
            value_ref[...],
            error_ref[...],
            (((0,), (0,)), ((), ())),
            preferred_element_type=jnp.float32,
        ).astype(out_ref.dtype)

    def clear():
        out_ref[...] = jnp.zeros_like(out_ref)

    each_layer(top_ref[0], (own_ref, far_ref, near_ref), multiply, clear)


def gradients(top, me, values, halves, start, width, depth, bits, held, after):
    layers = sum(x.shape[0] for x in values)
    tokens, features = values[0].shape[1:]
    pieces = len(halves)
    piece = width // pieces
    first = start // width
    operands = [top, me, *map(in_vmem, values)] + [near for near, _ in halves] + [far for _, far in halves]
    in_specs = [WHOLE] * 3 + [pl.BlockSpec((tokens // 2, piece), lambda s, top, me: (0, 0))] * (2 * pieces)
    operands.append(after)
    in_specs.append(pl.BlockSpec(memory_space=pl.ANY))
    aliases = {}
    if held is not None:
        aliases = {len(operands): 0}
        operands.append(held)
        in_specs.append(pl.BlockSpec(memory_space=pl.ANY))
    return pl.pallas_call(
        functools.partial(grad_kernel, bits, pieces),
        grid_spec=pltpu.PrefetchScalarGridSpec(
            num_scalar_prefetch=2,
            grid=(layers,),
            in_specs=in_specs,
            out_specs=[
                pl.BlockSpec(
                    (1, features, width), lambda s, top, me: (layer_at(top[0], s), 0, first)
                ),
                pl.BlockSpec((ROWS, LANES), lambda s, top, me: (0, 0)),
            ],
            scratch_shapes=[pltpu.VMEM((tokens, width), jnp.bfloat16)],
        ),
        out_shape=[
            jax.ShapeDtypeStruct((layers, features, depth), jnp.bfloat16),
            jax.ShapeDtypeStruct((ROWS, LANES), jnp.float32),
        ],
        input_output_aliases=aliases,
        compiler_params=params(),
        cost_estimate=pl.CostEstimate(
            flops=2 * layers * tokens * features * width,
            bytes_accessed=2 * layers * features * (tokens + width),
            transcendentals=0,
        ),
    )(*operands)


def ordered(kernel, operands, specs, out_shape, after):
    def run(*refs):
        kernel(*refs[: len(operands)], *refs[len(operands) + 1 :])

    return pl.pallas_call(
        run,
        grid=(1,),
        in_specs=specs + [pl.BlockSpec(memory_space=pl.ANY)],
        out_specs=[pl.BlockSpec(x.shape, lambda i: (0, 0)) for x in out_shape],
        out_shape=out_shape,
        compiler_params=params(SMALL_BYTES),
        cost_estimate=pl.CostEstimate(flops=1000, bytes_accessed=1 << 20, transcendentals=0),
    )(*operands, after)


def columns_of(x, width, at):
    return pl.BlockSpec((x.shape[0], width), lambda i: (0, at))


def split(keep, arrived, parts, after):
    rows, width = keep.shape[0] // parts, keep.shape[1]

    def kernel(*refs):
        keep_ref, arrived_refs = refs[0], refs[1 : 1 + len(arrived)]
        for part, out_ref in enumerate(refs[1 + len(arrived) :]):
            at = slice(part * rows, (part + 1) * rows)
            total = keep_ref[at, :]
            for arrived_ref in arrived_refs:
                total = total + arrived_ref[at, :].astype(jnp.float32)
            out_ref[...] = total.astype(out_ref.dtype)

    operands = [keep, *arrived]
    outs = ordered(
        kernel,
        operands,
        [columns_of(x, width, 0) for x in operands],
        [jax.ShapeDtypeStruct((rows, width), jnp.float32)]
        + [jax.ShapeDtypeStruct((rows, width), jnp.bfloat16)] * (parts - 1),
        after,
    )
    return outs[0], outs[1:]


def error_of(keep, arrived, bias, target, at, after):
    rows, width = keep.shape

    def kernel(bias_ref, target_ref, keep_ref, *refs):
        total = keep_ref[...]
        for arrived_ref in refs[:-2]:
            total = total + arrived_ref[...].astype(jnp.float32)
        error = total + bias_ref[...] - target_ref[...].astype(jnp.float32)
        refs[-2][...] = error
        refs[-1][...] = error.astype(jnp.bfloat16)

    return ordered(
        kernel,
        [bias, target, keep, *arrived],
        [columns_of(bias, width, at), columns_of(target, width, at)]
        + [columns_of(x, width, 0) for x in [keep, *arrived]],
        [
            jax.ShapeDtypeStruct((rows, width), jnp.float32),
            jax.ShapeDtypeStruct((rows, width), jnp.bfloat16),
        ],
        after,
    )


def joined(arrays, after):
    rows, width = arrays[0].shape

    def kernel(*refs):
        for i, ref in enumerate(refs[:-1]):
            refs[-1][i * rows : (i + 1) * rows, :] = ref[...]

    return ordered(
        kernel,
        arrays,
        [columns_of(x, width, 0) for x in arrays],
        [jax.ShapeDtypeStruct((rows * len(arrays), width), jnp.bfloat16)],
        after,
    )[0]


def local(resid, enc_weight, enc_bias, active, dec_weight, dec_bias, target):
    features = enc_weight.shape[2]
    layers = dec_weight.shape[1]
    tokens, depth = resid.shape[1:]
    slots = active.shape[2]
    shards = lax.axis_size("feat")
    bits = shards.bit_length() - 1
    rows = tokens // shards
    feat_index = lax.axis_index("feat")
    pair_index = lax.axis_index("pair")
    top = pair_index.astype(jnp.int32).reshape(1)
    me = feat_index.astype(jnp.int32).reshape(1)

    offset = active[0] - feat_index * features
    inside = (offset >= 0) & (offset < features)
    slot_index = jnp.sort(jnp.where(inside, offset, FAR), axis=1)

    def folded(x):
        x = x.reshape(tokens // ROWS, ROWS, slots // SLOTS, SLOTS)
        return x.transpose(0, 2, 1, 3).reshape(tokens // ROWS, ROWS * slots)

    def across(x, step):
        return lax.ppermute(x, "pair", [(i, i ^ step) for i in range(layers)])

    far_step, near_step = layers // 2, 1
    own_index = folded(slot_index)
    own_short = own_index.astype(jnp.int16)
    far_short = across(own_short, far_step)
    own_value = folded(encode(resid[0], enc_weight[0], enc_bias, slot_index))
    far_value = across(own_value, far_step)

    def pack(*xs):
        return jnp.stack(xs)

    def wide(x):
        return x.astype(jnp.float32 if x.dtype == jnp.bfloat16 else jnp.int32)

    own = spread(top, (0,), own_index[None], wide(own_value)[None], features)
    near_short = across(pack(own_short, far_short), near_step)
    near_value = across(pack(own_value, far_value), near_step)
    far = spread(top, (far_step,), wide(far_short)[None], wide(far_value)[None], features)
    near = spread(
        top, (near_step, near_step + far_step), wide(near_short), wide(near_value), features
    )
    values = (own, far, near)

    def swap(parts, group):
        masks = [
            sum(((part >> j) & 1) << group[-1 - j] for j in range(len(group)))
            for part in range(1, 1 << len(group))
        ]
        return [
            lax.ppermute(x, "feat", [(i, i ^ mask) for i in range(shards)])
            for x, mask in zip(parts, masks)
        ]

    piece = min(PIECE, depth)
    count = depth // piece
    last = top
    grads = None
    state = [None] * count
    halves = [None] * count
    errors = [None] * count

    def rebuild_step(p):
        nonlocal last
        ((keep, last),) = rebuild(
            top, me, values, dec_weight[0], p * piece, piece, piece, bits, last
        )
        state[p] = (keep, swap([last], (0,)))

    def reduce_step(p, group):
        nonlocal last
        keep, sends = split(*state[p], 1 << len(group), last)
        last = sends[-1]
        state[p] = (keep, swap(sends, group))

    def error_step(p, group):
        nonlocal last
        errors[p], last = error_of(*state[p], dec_bias, target[0], p, last)
        state[p] = (last, swap([last] * ((1 << len(group)) - 1), group))

    def gather_step(p, group):
        nonlocal last
        last = joined([state[p][0], *state[p][1]], last)
        state[p] = (last, swap([last] * ((1 << len(group)) - 1), group))

    def grad_step(p):
        nonlocal grads, last
        near, (far,) = state[p]
        grads, last = gradients(
            top, me, values, [(near, far)], p * piece, piece, depth, bits, grads, last
        )

    def steps_of(p, down, up):
        steps = [functools.partial(reduce_step, p, group) for group in down]
        steps.append(functools.partial(error_step, p, up[0]))
        steps += [functools.partial(gather_step, p, group) for group in [*up[1:], (0,)]]
        return steps

    if count == len(GROUPS) and bits == 3:
        groups = GROUPS
        plan = PLAN
    else:
        ones = [(bit,) for bit in range(1, bits)]
        groups = [(ones, ones[::-1])] * count
        plan = [(p, REBUILD) for p in range(count)]
        plan += [(p, i) for i in range(2 * bits - 1) for p in range(count)]
        plan += [(p, GRADIENT) for p in range(count)]
    steps = [steps_of(p, *groups[p]) for p in range(count)]
    for p, i in plan:
        if i == REBUILD:
            rebuild_step(p)
        elif i == GRADIENT:
            grad_step(p)
        else:
            steps[p][i]()
    error = jnp.concatenate(errors, axis=1)
    return (error[None], grads[None])


def solution(mesh):
    in_specs = (
        P("pair", None, None),
        P("pair", None, "feat"),
        P("pair", "feat"),
        P("pair", None, None),
        P("pair", None, "feat", None),
        P("pair", None),
        P("pair", "feat", None),
    )
    out_specs = (P("pair", "feat", None), P("pair", None, "feat", None))
    return jax.shard_map(local, mesh=mesh, in_specs=in_specs, out_specs=out_specs, check_vma=False)
```

```python
import functools

import jax
import jax.numpy as jnp
from jax import lax
from jax.experimental import pallas as pl
from jax.experimental.pallas import tpu as pltpu
from jax.sharding import PartitionSpec as P

LANES = 128
ROWS = 8
SLOTS = 32
FAR = 32767
ENCODE_BYTES = 56 * 1024 * 1024
VMEM_BYTES = 24 * 1024 * 1024
SMALL_BYTES = 8 * 1024 * 1024
PIECE = 512
GROUPS = (
    (((1,), (2,)), ((2,), (1,))),
    (((1,), (2,)), ((2,), (1,))),
    (((1,), (2,)), ((2,), (1,))),
    (((1,), (2,)), ((2,), (1,))),
)
REBUILD, GRADIENT = -1, -2
PLAN = (
    (0, REBUILD), (1, REBUILD), (0, 0), (2, REBUILD), (0, 1), (1, 0), (3, REBUILD), (0, 2), (1, 1),
    (2, 0), (0, 3), (1, 2), (2, 1), (0, 4), (3, 0), (1, 3), (2, 2), (3, 1), (1, 4), (2, 3), (3, 2),
    (0, GRADIENT), (2, 4), (3, 3), (1, GRADIENT), (3, 4), (2, GRADIENT), (3, GRADIENT),
)


WHOLE = pl.BlockSpec(memory_space=pltpu.VMEM)


def in_vmem(x):
    return pltpu.with_memory_space_constraint(x, pltpu.VMEM)


def params(limit=VMEM_BYTES):
    return pltpu.CompilerParams(vmem_limit_bytes=limit)


def encode_kernel(resid_ref, weight_ref, bias_ref, slot_ref, out_ref, pre_ref, picked_ref, index_ref):
    step = pl.program_id(0)
    tokens = resid_ref.shape[0]
    width = weight_ref.shape[1]
    slots = slot_ref.shape[1]
    groups = width // LANES

    @pl.when(step == 0)
    def _():
        picked_ref[...] = jnp.zeros_like(picked_ref)
        pre_ref[1] = jnp.zeros_like(pre_ref[1])
        index_ref[...] = jnp.full_like(index_ref, FAR)
        index_ref[:, :slots] = slot_ref[...]

    now = lax.rem(step, 2)
    before = 1 - now
    first = (step - 1) * groups

    def pick():
        for row in range(0, tokens, ROWS):
            rows = pl.ds(row, ROWS)
            index = index_ref[rows, :]
            group = (index >> 7) - first
            lane = index & (LANES - 1)
            picked = picked_ref[rows, :]
            for part in range(groups):
                source = pre_ref[before, rows, part * LANES : (part + 1) * LANES]
                found = jnp.take_along_axis(source, lane, axis=1)
                picked = jnp.where(group == part, found, picked)
            picked_ref[rows, :] = picked

    @pl.when(step < pl.num_programs(0) - 1)
    def _():
        pre_ref[now] = (
            jnp.dot(resid_ref[...], weight_ref[...], preferred_element_type=jnp.float32)
            + bias_ref[...]
        )
        pick()

    @pl.when(step == pl.num_programs(0) - 1)
    def _():
        pick()
        out_ref[...] = jnp.maximum(picked_ref[:, :slots], 0.0).astype(out_ref.dtype)


def encode(resid, weight, bias, slot_index):
    tokens, depth = resid.shape
    features = weight.shape[1]
    slots = slot_index.shape[1]
    width = min(256, features)
    steps = features // width
    return pl.pallas_call(
        encode_kernel,
        grid=(steps + 1,),
        in_specs=[
            WHOLE,
            pl.BlockSpec((depth, width), lambda i: (0, jnp.minimum(i, steps - 1))),
            pl.BlockSpec((1, width), lambda i: (0, jnp.minimum(i, steps - 1))),
            pl.BlockSpec((tokens, slots), lambda i: (0, 0)),
        ],
        out_specs=pl.BlockSpec((tokens, slots), lambda i: (0, 0)),
        out_shape=jax.ShapeDtypeStruct((tokens, slots), jnp.bfloat16),
        scratch_shapes=[
            pltpu.VMEM((2, tokens, width), jnp.float32),
            pltpu.VMEM((tokens, LANES), jnp.float32),
            pltpu.VMEM((tokens, LANES), jnp.int32),
        ],
        compiler_params=params(ENCODE_BYTES),
        cost_estimate=pl.CostEstimate(
            flops=2 * tokens * depth * features,
            bytes_accessed=2 * depth * (features + tokens),
            transcendentals=0,
        ),
    )(in_vmem(resid), weight, bias, slot_index)


def spread_kernel(places, top_ref, deep_ref, index_ref, value_ref, out_ref):
    at = pl.program_id(0)
    place = places[0] + at * (places[-1] - places[0])
    blocks = index_ref.shape[1]
    features = out_ref.shape[2]
    groups = features // LANES
    top = top_ref[0]
    source = jnp.bitwise_xor(top, place)
    span = ROWS * SLOTS

    def rows_of(block, rounds):
        high = lax.broadcasted_iota(jnp.int32, (groups * ROWS, span), 0)
        low = lax.broadcasted_iota(jnp.int32, (LANES, span), 0)
        token = lax.broadcasted_iota(jnp.int32, (1, span), 1) // SLOTS
        total = None
        for turn in range(rounds):
            part = pl.ds(turn * span, span)
            index = index_ref[0, pl.ds(block, 1), part]
            value = value_ref[0, pl.ds(block, 1), part]
            key = (index >> 7) * ROWS + token
            lane = index & (LANES - 1)
            left = jnp.where(
                jnp.broadcast_to(key, high.shape) == high, jnp.broadcast_to(value, high.shape), 0.0
            ).astype(jnp.bfloat16)
            right = jnp.where(jnp.broadcast_to(lane, low.shape) == low, 1.0, 0.0).astype(
                jnp.bfloat16
            )
            part = lax.dot_general(
                left, right, (((1,), (1,)), ((), ())), preferred_element_type=jnp.float32
            )
            total = part if total is None else total + part
        return total

    def run(rounds, unroll):
        def pair(i, carry):
            one, two = rows_of(2 * i, rounds), rows_of(2 * i + 1, rounds)
            first = (pl.program_id(1) * blocks + 2 * i) * ROWS
            rows = pl.ds(pl.multiple_of(first, 2 * ROWS), 2 * ROWS)
            for group in range(groups):
                part = slice(group * ROWS, (group + 1) * ROWS)
                out_ref[at, rows, group * LANES : (group + 1) * LANES] = jnp.concatenate(
                    [one[part], two[part]], axis=0
                ).astype(out_ref.dtype)
            return carry

        lax.fori_loop(0, blocks // 2, pair, 0, unroll=unroll)

    deep = deep_ref[at]

    @pl.when((source <= top) & (deep == 0))
    def _():
        run(1, 8)

    @pl.when((source <= top) & (deep != 0))
    def _():
        run(index_ref.shape[2] // span, 1)


def spread(top, places, index, value, features):
    count, blocks, wide = index.shape
    block = min(32, blocks)
    deep = jnp.any(index[:, :, ROWS * SLOTS :] != FAR, axis=(1, 2)).astype(jnp.int32)
    tokens = blocks * ROWS
    return pl.pallas_call(
        functools.partial(spread_kernel, places),
        grid_spec=pltpu.PrefetchScalarGridSpec(
            num_scalar_prefetch=2,
            grid=(count, blocks // block),
            in_specs=[pl.BlockSpec((1, block, wide), lambda p, b, top, deep: (p, b, 0))] * 2,
            out_specs=WHOLE,
        ),
        out_shape=pltpu.VMEM((count, tokens, features), jnp.bfloat16),
        compiler_params=params(),
        cost_estimate=pl.CostEstimate(
            flops=count * 2 * tokens * features * 32,
            bytes_accessed=count * tokens * features * 2,
            transcendentals=0,
        ),
    )(top, deep, index, value)


PLACES = (0, 2, 1, 3)


def layer_at(top, step):
    place = jnp.where(step == 0, 0, jnp.where(step == 1, PLACES[1], 2 * step - 3))
    return jnp.bitwise_xor(top, place)


def each_layer(top, value_refs, body, otherwise):
    own_ref, far_ref, near_ref = value_refs
    step = pl.program_id(0)
    used = layer_at(top, step) <= top

    @pl.when(step == 0)
    def _():
        body(own_ref.at[0], True)

    @pl.when((step == 1) & used)
    def _():
        body(far_ref.at[0], False)

    @pl.when((step > 1) & used)
    def _():
        body(near_ref.at[step - 2], False)

    if otherwise is not None:
        pl.when(jnp.logical_not(used))(otherwise)


def relative_block(me, place, bits):
    pattern = sum(((place >> j) & 1) << (bits - 1 - j) for j in range(bits))
    return jnp.bitwise_xor(me, pattern)


def rebuild_kernel(bits, top_ref, me_ref, own_ref, far_ref, near_ref, weight_ref, after_ref, *refs):
    keep_refs, send_refs, total_ref = refs[: len(refs) // 2], refs[len(refs) // 2 : -1], refs[-1]
    step = pl.program_id(0)

    def add(value_ref, first):
        product = jnp.dot(value_ref[...], weight_ref[0], preferred_element_type=jnp.float32)
        total_ref[...] = product if first else total_ref[...] + product

    each_layer(top_ref[0], (own_ref, far_ref, near_ref), add, None)

    @pl.when(step == pl.num_programs(0) - 1)
    def _():
        count = 1 << bits
        rows = total_ref.shape[0] // count
        half = count // 2
        width = keep_refs[0].shape[1]
        for place in range(count):
            start = pl.multiple_of(relative_block(me_ref[0], place, bits) * rows, rows)
            for piece in range(len(keep_refs)):
                block = total_ref[pl.ds(start, rows), piece * width : (piece + 1) * width]
                if place < half:
                    keep_refs[piece][place * rows : (place + 1) * rows, :] = block
                else:
                    at = (place - half) * rows
                    send_refs[piece][at : at + rows, :] = block.astype(jnp.bfloat16)


def rebuild(top, me, values, weight, start, width, piece, bits, after):
    layers = weight.shape[0]
    tokens, features = values[0].shape[1:]
    first = start // width
    pieces = width // piece
    shape = (tokens // 2, piece)
    outs = pl.pallas_call(
        functools.partial(rebuild_kernel, bits),
        grid_spec=pltpu.PrefetchScalarGridSpec(
            num_scalar_prefetch=2,
            grid=(layers,),
            in_specs=[
                WHOLE,
                WHOLE,
                WHOLE,
                pl.BlockSpec(
                    (1, features, width),
                    lambda s, top, me: (jnp.minimum(layer_at(top[0], s), top[0]), 0, first),
                ),
                pl.BlockSpec(memory_space=pl.ANY),
            ],
            out_specs=[pl.BlockSpec(shape, lambda s, top, me: (0, 0))] * (2 * pieces),
            scratch_shapes=[pltpu.VMEM((tokens, width), jnp.float32)],
        ),
        out_shape=[jax.ShapeDtypeStruct(shape, jnp.float32)] * pieces
        + [jax.ShapeDtypeStruct(shape, jnp.bfloat16)] * pieces,
        compiler_params=params(),
        cost_estimate=pl.CostEstimate(
            flops=2 * layers * tokens * features * width,
            bytes_accessed=2 * layers * features * (tokens + width),
            transcendentals=0,
        ),
    )(top, me, *map(in_vmem, values), weight, after)
    return list(zip(outs[:pieces], outs[pieces:]))


def grad_kernel(bits, pieces, top_ref, me_ref, own_ref, far_ref, near_ref, *refs):
    near_refs, far_refs = refs[:pieces], refs[pieces : 2 * pieces]
    out_ref, done_ref, error_ref = refs[-3:]
    source = pl.program_id(0)

    @pl.when(source == 0)
    def _():
        done_ref[...] = jnp.zeros_like(done_ref)
        count = 1 << bits
        rows = error_ref.shape[0] // count
        half = count // 2
        width = near_refs[0].shape[1]
        for place in range(count):
            start = pl.multiple_of(relative_block(me_ref[0], place, bits) * rows, rows)
            for piece in range(pieces):
                from_ref = near_refs[piece] if place < half else far_refs[piece]
                at = (place % half) * rows
                error_ref[pl.ds(start, rows), piece * width : (piece + 1) * width] = from_ref[
                    at : at + rows, :
                ]

    def multiply(value_ref, first):
        out_ref[0] = lax.dot_general(
            value_ref[...],
            error_ref[...],
            (((0,), (0,)), ((), ())),
            preferred_element_type=jnp.float32,
        ).astype(out_ref.dtype)

    def clear():
        out_ref[...] = jnp.zeros_like(out_ref)

    each_layer(top_ref[0], (own_ref, far_ref, near_ref), multiply, clear)


def gradients(top, me, values, halves, start, width, depth, bits, held, after):
    layers = sum(x.shape[0] for x in values)
    tokens, features = values[0].shape[1:]
    pieces = len(halves)
    piece = width // pieces
    first = start // width
    operands = [top, me, *map(in_vmem, values)] + [near for near, _ in halves] + [far for _, far in halves]
    in_specs = [WHOLE] * 3 + [pl.BlockSpec((tokens // 2, piece), lambda s, top, me: (0, 0))] * (2 * pieces)
    operands.append(after)
    in_specs.append(pl.BlockSpec(memory_space=pl.ANY))
    aliases = {}
    if held is not None:
        aliases = {len(operands): 0}
        operands.append(held)
        in_specs.append(pl.BlockSpec(memory_space=pl.ANY))
    return pl.pallas_call(
        functools.partial(grad_kernel, bits, pieces),
        grid_spec=pltpu.PrefetchScalarGridSpec(
            num_scalar_prefetch=2,
            grid=(layers,),
            in_specs=in_specs,
            out_specs=[
                pl.BlockSpec(
                    (1, features, width), lambda s, top, me: (layer_at(top[0], s), 0, first)
                ),
                pl.BlockSpec((ROWS, LANES), lambda s, top, me: (0, 0)),
            ],
            scratch_shapes=[pltpu.VMEM((tokens, width), jnp.bfloat16)],
        ),
        out_shape=[
            jax.ShapeDtypeStruct((layers, features, depth), jnp.bfloat16),
            jax.ShapeDtypeStruct((ROWS, LANES), jnp.float32),
        ],
        input_output_aliases=aliases,
        compiler_params=params(),
        cost_estimate=pl.CostEstimate(
            flops=2 * layers * tokens * features * width,
            bytes_accessed=2 * layers * features * (tokens + width),
            transcendentals=0,
        ),
    )(*operands)


def ordered(kernel, operands, specs, out_shape, after):
    def run(*refs):
        kernel(*refs[: len(operands)], *refs[len(operands) + 1 :])

    return pl.pallas_call(
        run,
        grid=(1,),
        in_specs=specs + [pl.BlockSpec(memory_space=pl.ANY)],
        out_specs=[pl.BlockSpec(x.shape, lambda i: (0, 0)) for x in out_shape],
        out_shape=out_shape,
        compiler_params=params(SMALL_BYTES),
        cost_estimate=pl.CostEstimate(flops=1000, bytes_accessed=1 << 20, transcendentals=0),
    )(*operands, after)


def columns_of(x, width, at):
    return pl.BlockSpec((x.shape[0], width), lambda i: (0, at))


def split(keep, arrived, parts, after):
    rows, width = keep.shape[0] // parts, keep.shape[1]

    def kernel(*refs):
        keep_ref, arrived_refs = refs[0], refs[1 : 1 + len(arrived)]
        for part, out_ref in enumerate(refs[1 + len(arrived) :]):
            at = slice(part * rows, (part + 1) * rows)
            total = keep_ref[at, :]
            for arrived_ref in arrived_refs:
                total = total + arrived_ref[at, :].astype(jnp.float32)
            out_ref[...] = total.astype(out_ref.dtype)

    operands = [keep, *arrived]
    outs = ordered(
        kernel,
        operands,
        [columns_of(x, width, 0) for x in operands],
        [jax.ShapeDtypeStruct((rows, width), jnp.float32)]
        + [jax.ShapeDtypeStruct((rows, width), jnp.bfloat16)] * (parts - 1),
        after,
    )
    return outs[0], outs[1:]


def error_of(keep, arrived, bias, target, at, after):
    rows, width = keep.shape

    def kernel(bias_ref, target_ref, keep_ref, *refs):
        total = keep_ref[...]
        for arrived_ref in refs[:-2]:
            total = total + arrived_ref[...].astype(jnp.float32)
        error = total + bias_ref[...] - target_ref[...].astype(jnp.float32)
        refs[-2][...] = error
        refs[-1][...] = error.astype(jnp.bfloat16)

    return ordered(
        kernel,
        [bias, target, keep, *arrived],
        [columns_of(bias, width, at), columns_of(target, width, at)]
        + [columns_of(x, width, 0) for x in [keep, *arrived]],
        [
            jax.ShapeDtypeStruct((rows, width), jnp.float32),
            jax.ShapeDtypeStruct((rows, width), jnp.bfloat16),
        ],
        after,
    )


def joined(arrays, after):
    rows, width = arrays[0].shape

    def kernel(*refs):
        for i, ref in enumerate(refs[:-1]):
            refs[-1][i * rows : (i + 1) * rows, :] = ref[...]

    return ordered(
        kernel,
        arrays,
        [columns_of(x, width, 0) for x in arrays],
        [jax.ShapeDtypeStruct((rows * len(arrays), width), jnp.bfloat16)],
        after,
    )[0]


def local(resid, enc_weight, enc_bias, active, dec_weight, dec_bias, target):
    features = enc_weight.shape[2]
    layers = dec_weight.shape[1]
    tokens, depth = resid.shape[1:]
    slots = active.shape[2]
    shards = lax.axis_size("feat")
    bits = shards.bit_length() - 1
    rows = tokens // shards
    feat_index = lax.axis_index("feat")
    pair_index = lax.axis_index("pair")
    top = pair_index.astype(jnp.int32).reshape(1)
    me = feat_index.astype(jnp.int32).reshape(1)

    offset = active[0] - feat_index * features
    inside = (offset >= 0) & (offset < features)
    slot_index = jnp.sort(jnp.where(inside, offset, FAR), axis=1)

    def folded(x):
        x = x.reshape(tokens // ROWS, ROWS, slots // SLOTS, SLOTS)
        return x.transpose(0, 2, 1, 3).reshape(tokens // ROWS, ROWS * slots)

    def across(x, step):
        return lax.ppermute(x, "pair", [(i, i ^ step) for i in range(layers)])

    far_step, near_step = layers // 2, 1
    own_index = folded(slot_index)
    own_short = own_index.astype(jnp.int16)
    far_short = across(own_short, far_step)
    own_value = folded(encode(resid[0], enc_weight[0], enc_bias, slot_index))
    far_value = across(own_value, far_step)

    def pack(*xs):
        return jnp.stack(xs)

    def wide(x):
        return x.astype(jnp.float32 if x.dtype == jnp.bfloat16 else jnp.int32)

    own = spread(top, (0,), own_index[None], wide(own_value)[None], features)
    near_short = across(pack(own_short, far_short), near_step)
    near_value = across(pack(own_value, far_value), near_step)
    far = spread(top, (far_step,), wide(far_short)[None], wide(far_value)[None], features)
    near = spread(
        top, (near_step, near_step + far_step), wide(near_short), wide(near_value), features
    )
    values = (own, far, near)

    def swap(parts, group):
        masks = [
            sum(((part >> j) & 1) << group[-1 - j] for j in range(len(group)))
            for part in range(1, 1 << len(group))
        ]
        return [
            lax.ppermute(x, "feat", [(i, i ^ mask) for i in range(shards)])
            for x, mask in zip(parts, masks)
        ]

    piece = min(PIECE, depth)
    count = depth // piece
    last = top
    grads = None
    state = [None] * count
    halves = [None] * count
    errors = [None] * count

    def rebuild_step(p):
        nonlocal last
        ((keep, last),) = rebuild(
            top, me, values, dec_weight[0], p * piece, piece, piece, bits, last
        )
        state[p] = (keep, swap([last], (0,)))

    def reduce_step(p, group):
        nonlocal last
        keep, sends = split(*state[p], 1 << len(group), last)
        last = sends[-1]
        state[p] = (keep, swap(sends, group))

    def error_step(p, group):
        nonlocal last
        errors[p], last = error_of(*state[p], dec_bias, target[0], p, last)
        state[p] = (last, swap([last] * ((1 << len(group)) - 1), group))

    def gather_step(p, group):
        nonlocal last
        last = joined([state[p][0], *state[p][1]], last)
        state[p] = (last, swap([last] * ((1 << len(group)) - 1), group))

    def grad_step(p):
        nonlocal grads, last
        near, (far,) = state[p]
        grads, last = gradients(
            top, me, values, [(near, far)], p * piece, piece, depth, bits, grads, last
        )

    def steps_of(p, down, up):
        steps = [functools.partial(reduce_step, p, group) for group in down]
        steps.append(functools.partial(error_step, p, up[0]))
        steps += [functools.partial(gather_step, p, group) for group in [*up[1:], (0,)]]
        return steps

    if count == len(GROUPS) and bits == 3:
        groups = GROUPS
        plan = PLAN
    else:
        ones = [(bit,) for bit in range(1, bits)]
        groups = [(ones, ones[::-1])] * count
        plan = [(p, REBUILD) for p in range(count)]
        plan += [(p, i) for i in range(2 * bits - 1) for p in range(count)]
        plan += [(p, GRADIENT) for p in range(count)]
    steps = [steps_of(p, *groups[p]) for p in range(count)]
    for p, i in plan:
        if i == REBUILD:
            rebuild_step(p)
        elif i == GRADIENT:
            grad_step(p)
        else:
            steps[p][i]()
    error = jnp.concatenate(errors, axis=1)
    return (error[None], grads[None])


def solution(mesh):
    in_specs = (
        P("pair", None, None),
        P("pair", None, "feat"),
        P("pair", "feat"),
        P("pair", None, None),
        P("pair", None, "feat", None),
        P("pair", None),
        P("pair", "feat", None),
    )
    out_specs = (P("pair", "feat", None), P("pair", None, "feat", None))
    return jax.shard_map(local, mesh=mesh, in_specs=in_specs, out_specs=out_specs, check_vma=False)
```
